32 devices in a mesh: vrow: 2 (over y), vcol: 2 (over x), pix: 8 (over z, core).
Axes of the slice: x: 2, y: 2, z: 4, core: 2. Of those that a mesh axis runs over, the one named last changes fastest.
Arguments:
- features: bfloat16 [16, 16, 64, 1024], P('vrow', 'vcol', None, 'pix'), may hold values from -400 to 400
- out_cotangent: bfloat16 [16, 16, 64, 1024], P('vrow', 'vcol', None, 'pix'), may hold values from -6 to 6
- norm_gain: float32 [64], replicated, may hold values from 0.25 to 1.75
- query_proj: bfloat16 [64, 64], replicated, may hold values from -0.75 to 0.75
- keyval_proj: bfloat16 [64, 128], replicated, may hold values from -0.75 to 0.75
- output_proj: bfloat16 [64, 64], replicated, may hold values from -0.75 to 0.75
Outputs:
- features_grad: bfloat16 [16, 16, 64, 1024], P('vrow', 'vcol', None, 'pix')
- query_proj_grad: float32 [64, 64], replicated
- keyval_proj_grad: float32 [64, 128], replicated
- output_proj_grad: float32 [64, 64], replicated
- norm_gain_grad: float32 [64], replicated
The draws below stay inside these ranges and needn't reach their ends.
All inputs are finite; a program needn't handle non-finite values.
Results may differ from the reference program's by a relative error of at most 0.0085.
Values may be sent and summed in bfloat16 or wider, within the bound.
A program may use at most 128 MiB of HBM per device.

```python
import math
import jax
import jax.numpy as jnp
from jax import lax

D = 64
HEADS = 4
VIEW_ROWS = 16
VIEW_COLS = 16
PIX_DEV = 128
PIXELS = 1024
TOKENS = 262144


def draw_features(key, part):
    noise_key, token_key, channel_key = jax.random.split(key, 3)
    full_shape = (VIEW_ROWS, VIEW_COLS, D, PIXELS)
    base_noise = jnp.clip(jax.random.normal(noise_key, full_shape, jnp.float32), -4.0, 4.0)
    token_scale = jnp.exp(jax.random.uniform(token_key, (VIEW_ROWS, VIEW_COLS, 1, PIXELS), jnp.float32) * math.log(10.0))
    channel_scale = jnp.exp(jax.random.uniform(channel_key, (1, 1, D, 1), jnp.float32) * math.log(10.0))
    return (base_noise * token_scale * channel_scale).astype(jnp.bfloat16)


def levels(stream_key, dims, shards, low, largest):
    level, own = 1.0, jax.random.fold_in(stream_key, 6)
    for axis_at, blocks in shards:
        steps = jnp.exp(jax.random.uniform(jax.random.fold_in(own, axis_at), (blocks,), jnp.float32, low / len(shards), largest / len(shards)))
        level = level * jnp.repeat(steps, dims[axis_at] // blocks).reshape([-1 if axis == axis_at else 1 for axis in range(len(dims))])
    return level


def centred(stream_key, extent, width, most, cuts=(), kind=jnp.bfloat16):
    entries = width * jax.random.normal(stream_key, extent, jnp.float32)
    if cuts:
        entries = entries * levels(stream_key, extent, cuts, -0.22, 0.18)
    return jnp.clip(entries, -most, most).astype(kind)


def setup_inputs(seed: int = 0) -> dict:
    key_list = jax.random.split(jax.random.key(seed), 7)
    features = draw_features(jax.random.fold_in(key_list[6], 71), 0)
    out_cotangent = centred(key_list[1], (VIEW_ROWS, VIEW_COLS, D, PIXELS), 1.0, 6.0, ((0, 2), (1, 2), (3, 8)))
    norm_gain = jnp.clip(1.0 + 0.15 * jax.random.normal(key_list[2], (D,), jnp.float32), 0.25, 1.75)
    query_proj = centred(key_list[3], (D, D), D ** -0.5, 0.75)
    keyval_proj = centred(key_list[4], (D, 2 * D), D ** -0.5, 0.75)
    output_proj = centred(key_list[5], (D, D), D ** -0.5, 0.75)
    return dict(features=features, out_cotangent=out_cotangent, norm_gain=norm_gain, query_proj=query_proj, keyval_proj=keyval_proj, output_proj=output_proj)


EPSILON = 1e-06
precise = lax.Precision.HIGHEST

def normalize(features, norm_gain):
    values = features.astype(jnp.float32)
    inv_norm = lax.rsqrt(lax.optimization_barrier(jnp.mean(values * values, axis=2, keepdims=True)) + EPSILON)
    scaled = values * inv_norm
    normed = (scaled * norm_gain[None, None, :, None]).astype(jnp.bfloat16)
    return (normed, scaled, inv_norm)

def unit_rows(raw_proj):
    inv_norm = lax.rsqrt(lax.optimization_barrier(jnp.mean(raw_proj * raw_proj, axis=2, keepdims=True)) + EPSILON)
    return (raw_proj * inv_norm, inv_norm)

def unit_back(unit_vals, inv_norm, upstream):
    return inv_norm * (upstream - unit_vals * lax.optimization_barrier(jnp.mean(upstream * unit_vals, axis=2, keepdims=True)))

def project(normed, weight):
    return jnp.einsum('uvdp,de->uvep', normed.astype(jnp.float32), weight.astype(jnp.float32), precision=precise)

def attention(query, keyval_pad):
    view_rows, view_cols, channels, pixels = query.shape
    head_size = channels // HEADS
    query_heads = query.reshape(view_rows, view_cols, HEADS, head_size, pixels)
    exp_total = jnp.zeros((view_rows, view_cols, HEADS, pixels), jnp.float32)
    weighted = jnp.zeros(query_heads.shape, jnp.float32)
    for row_shift in range(5):
        for col_shift in range(5):
            window = keyval_pad[row_shift:row_shift + view_rows, col_shift:col_shift + view_cols]
            key_heads = window[:, :, :channels].reshape(query_heads.shape)
            values = window[:, :, channels:].reshape(query_heads.shape)
            weight = jnp.exp(lax.optimization_barrier(jnp.sum(query_heads * key_heads, axis=3)) * head_size ** (-0.5))
            exp_total = exp_total + weight
            weighted = weighted + weight[:, :, :, None] * values
    return (weighted / exp_total[:, :, :, None]).reshape(view_rows, view_cols, channels, pixels)

def block_pass(features, cotangent, norm_gain, query_proj, keyval_proj, output_proj):
    normed, scaled, inv_norm = normalize(features, norm_gain)
    channels = features.shape[2]
    raw_query = project(normed, query_proj)
    unit_query, query_inv = unit_rows(raw_query)
    query = lax.optimization_barrier(unit_query.astype(jnp.bfloat16)).astype(jnp.float32)
    raw_keyval = project(normed, keyval_proj)
    unit_key, key_inv = unit_rows(raw_keyval[:, :, :channels])
    keyval = jnp.concatenate([unit_key, raw_keyval[:, :, channels:]], axis=2)
    keyval = lax.optimization_barrier(keyval.astype(jnp.bfloat16)).astype(jnp.float32)
    keyval_pad = jnp.pad(keyval, ((2, 2), (2, 2), (0, 0), (0, 0)))
    attended, pullback = jax.vjp(attention, query, keyval_pad)
    mixed_out = attended.astype(jnp.bfloat16)
    cot_float = cotangent.astype(jnp.float32)
    out_grad = jnp.einsum('uvep,de->uvdp', cot_float, output_proj.astype(jnp.float32), precision=precise)
    query_grad, keyval_pad_grad = pullback(out_grad)
    keyval_grad = keyval_pad_grad[2:-2, 2:-2]
    raw_query_grad = unit_back(unit_query, query_inv, query_grad)
    raw_keyval_grad = jnp.concatenate([unit_back(unit_key, key_inv, keyval_grad[:, :, :channels]), keyval_grad[:, :, channels:]], axis=2)
    normed_grad = jnp.einsum('uvep,de->uvdp', raw_query_grad, query_proj.astype(jnp.float32), precision=precise)
    normed_grad = normed_grad + jnp.einsum('uvep,de->uvdp', raw_keyval_grad, keyval_proj.astype(jnp.float32), precision=precise)
    normed_float = normed.astype(jnp.float32)
    query_part = jnp.einsum('uvdp,uvep->de', normed_float, raw_query_grad, precision=precise)
    keyval_part = jnp.einsum('uvdp,uvep->de', normed_float, raw_keyval_grad, precision=precise)
    output_part = jnp.einsum('uvdp,uvep->de', mixed_out.astype(jnp.float32), cot_float, precision=precise)
    scaled_grad = normed_grad * norm_gain[None, None, :, None]
    gain_part = lax.optimization_barrier(jnp.sum(normed_grad * scaled, axis=(0, 1, 3)))
    branch = inv_norm * (scaled_grad - scaled * lax.optimization_barrier(jnp.mean(scaled_grad * scaled, axis=2, keepdims=True)))
    features_grad = (cot_float + branch).astype(jnp.bfloat16)
    return (features_grad, (query_part, keyval_part, output_part, gain_part))

def reference(features, out_cotangent, norm_gain, query_proj, keyval_proj, output_proj):
    block_size = min(PIX_DEV, 128)
    block_count = PIXELS // block_size

    def scan_step(weight_sums, block_index):
        first_pixel = (block_index * block_size).astype(jnp.int32)
        feature_block = lax.dynamic_slice_in_dim(features, first_pixel, block_size, 3)
        cotangent_block = lax.dynamic_slice_in_dim(out_cotangent, first_pixel, block_size, 3)
        grad_block, parts = block_pass(feature_block, cotangent_block, norm_gain, query_proj, keyval_proj, output_proj)
        return (tuple((summed + addend for summed, addend in zip(weight_sums, parts))), grad_block)
    initial = (jnp.zeros((D, D), jnp.float32), jnp.zeros((D, 2 * D), jnp.float32), jnp.zeros((D, D), jnp.float32), jnp.zeros((D,), jnp.float32))
    weight_sums, grad_blocks = lax.scan(scan_step, initial, jnp.arange(block_count, dtype=jnp.int32))
    features_grad = jnp.moveaxis(grad_blocks, 0, 3).reshape(VIEW_ROWS, VIEW_COLS, D, PIXELS)
    factor = 1.0 / math.sqrt(TOKENS)
    return (features_grad, weight_sums[0] * factor, weight_sums[1] * factor, weight_sums[2] * factor, weight_sums[3] * factor)
```

```python
import functools
import math

import jax
import jax.numpy as jnp
from jax import lax
from jax.experimental import pallas as pl
from jax.experimental.pallas import tpu as pltpu
from jax.sharding import PartitionSpec as P

HEADS = 4
REACH = 2
SPAN = 2 * REACH + 1
EPSILON = 1e-06
f32, bf16 = jnp.float32, jnp.bfloat16


def shift(block, axis, up):
    count = lax.axis_size(axis)
    pairs = [(i, i + 1) if up else (i + 1, i) for i in range(count - 1)]
    return lax.ppermute(block, axis, pairs)


def lanes(ref, row, cols):
    return jnp.concatenate([ref[row, c] for c in cols], axis=1)


def unit_inv(raw):
    return lax.rsqrt(jnp.mean(raw * raw, axis=0, keepdims=True) + EPSILON)


def matmul(a, b):
    return jnp.dot(a, b, preferred_element_type=f32)


def matmul_nt(a, b):
    return lax.dot_general(a, b, (((1,), (1,)), ((), ())), preferred_element_type=f32)


def normalized(x, gain):
    inv = lax.rsqrt(jnp.mean(x * x, axis=0, keepdims=True) + EPSILON)
    scaled = x * inv
    return (scaled * gain).astype(bf16), scaled, inv


def attend_kernel(
    feat, cot, gain, w_t, wo, dq_out, att_out, dkv_out, q_s, g_s, kv_s, dkv_s, w_s, dp_s, dq_s, att_s
):
    rows, cols, chans, pix = cot.shape
    rows_p, cols_p = feat.shape[:2]
    size = chans // HEADS
    scale = size ** (-0.5)
    kv_row = 2 * chans * cols_p
    q_row = chans * cols
    own = range(REACH, REACH + cols)

    def front(row, _):
        x = lanes(feat, row, range(cols_p)).astype(f32)
        normed, _, _ = normalized(x, gain[...])
        raw = matmul(w_t[...], normed)
        raw_q, raw_k, value = raw[:chans], raw[chans : 2 * chans], raw[2 * chans :]
        query = (raw_q * unit_inv(raw_q)).astype(bf16).astype(f32)
        key = (raw_k * unit_inv(raw_k)).astype(bf16).astype(f32)
        value = value.astype(bf16).astype(f32)
        for c in range(cols_p):
            at = slice(c * pix, (c + 1) * pix)
            kv_s[pl.ds(row * kv_row + c, chans, stride=cols_p), :] = key[:, at]
            kv_s[pl.ds(row * kv_row + chans * cols_p + c, chans, stride=cols_p), :] = value[:, at]
        for i, c in enumerate(own):
            q_s[pl.ds(row * q_row + i, chans, stride=cols), :] = query[:, c * pix : (c + 1) * pix]
        dkv_s[pl.ds(row * kv_row, kv_row), :] = jnp.zeros((kv_row, pix), f32)
        return 0

    lax.fori_loop(0, rows_p, front, 0)

    def grads(row, _):
        out_grad = matmul(wo[...], lanes(cot, row, range(cols)))
        for i in range(cols):
            g_s[pl.ds(row * q_row + i, chans, stride=cols), :] = out_grad[:, i * pix : (i + 1) * pix]
        return 0

    lax.fori_loop(0, rows, grads, 0)

    def one(step, _):
        row, head = step // HEADS, step % HEADS
        q_at = (row + REACH) * q_row + head * size * cols
        g_at = row * q_row + head * size * cols
        q = [q_s[pl.ds(q_at + c * cols, cols), :] for c in range(size)]
        g = [g_s[pl.ds(g_at + c * cols, cols), :] for c in range(size)]
        v_off = chans * cols_p

        def fold(parts):
            while len(parts) > 1:
                parts = [a + b for a, b in zip(parts[::2], parts[1::2])]
            return parts[0]

        def forward(a, carry):
            total, w_dp, att = carry
            base = (row + a) * kv_row + head * size * cols_p
            for b in range(SPAN):
                def k(c):
                    return kv_s[pl.ds(base + (b + c * cols_p), cols), :]

                def v(c):
                    return kv_s[pl.ds(base + (v_off + b + c * cols_p), cols), :]

                w = jnp.exp(fold([q[c] * k(c) for c in range(size)]) * scale)
                dp = fold([g[c] * v(c) for c in range(size)])
                att = [att[c] + w * v(c) for c in range(size)]
                total = total + w
                w_dp = w_dp + w * dp
                at = pl.ds((a * SPAN + b) * cols, cols)
                w_s[at, :] = w
                dp_s[at, :] = dp
            return total, w_dp, att

        zero = jnp.zeros((cols, pix), f32)
        total, w_dp, att = lax.fori_loop(0, SPAN, forward, (zero, zero, [zero] * size))
        inv = 1.0 / total
        spread = w_dp * inv
        for c in range(size):
            att_s[pl.ds(g_at + c * cols, cols), :] = att[c] * inv

        def back(a, dq):
            base = (row + a) * kv_row + head * size * cols_p
            for b in range(SPAN):
                at = pl.ds((a * SPAN + b) * cols, cols)
                p = w_s[at, :] * inv
                ds = p * (dp_s[at, :] - spread) * scale
                dq = [dq[c] + ds * kv_s[pl.ds(base + (b + c * cols_p), cols), :] for c in range(size)]
                for c in range(size):
                    dkv_s[pl.ds(base + (b + c * cols_p), cols), :] += ds * q[c]
                for c in range(size):
                    dkv_s[pl.ds(base + (v_off + b + c * cols_p), cols), :] += p * g[c]
            return dq

        dq = lax.fori_loop(0, SPAN, back, [zero] * size)
        for c in range(size):
            dq_s[pl.ds(g_at + c * cols, cols), :] = dq[c]
        return 0

    lax.fori_loop(0, rows * HEADS, one, 0)

    def finish(row, _):
        for i in range(cols):
            dq_out[row, i] = dq_s[pl.ds(row * q_row + i, chans, stride=cols), :].astype(bf16)
            att_out[row, i] = att_s[pl.ds(row * q_row + i, chans, stride=cols), :].astype(bf16)
        return 0

    lax.fori_loop(0, rows, finish, 0)

    def finish_kv(row, _):
        for c in range(cols_p):
            dkv_out[row, c] = dkv_s[pl.ds(row * kv_row + c, 2 * chans, stride=cols_p), :].astype(bf16)
        return 0

    lax.fori_loop(0, rows_p, finish_kv, 0)


def attend(feat_pad, cot, gain, w_t, wo):
    rows, cols, chans, pix = cot.shape
    rows_p, cols_p = feat_pad.shape[:2]
    own = rows * chans * cols
    pad_kv = rows_p * 2 * chans * cols_p
    whole = pl.BlockSpec(memory_space=pltpu.VMEM)
    return pl.pallas_call(
        attend_kernel,
        out_shape=(
            jax.ShapeDtypeStruct(cot.shape, bf16),
            jax.ShapeDtypeStruct(cot.shape, bf16),
            jax.ShapeDtypeStruct((rows_p, cols_p, 2 * chans, pix), bf16),
        ),
        in_specs=[whole] * 5,
        out_specs=(whole,) * 3,
        scratch_shapes=[
            pltpu.VMEM((rows_p * chans * cols, pix), f32),
            pltpu.VMEM((own, pix), f32),
            pltpu.VMEM((pad_kv, pix), f32),
            pltpu.VMEM((pad_kv, pix), f32),
            pltpu.VMEM((SPAN * SPAN * cols, pix), f32),
            pltpu.VMEM((SPAN * SPAN * cols, pix), f32),
            pltpu.VMEM((own, pix), f32),
            pltpu.VMEM((own, pix), f32),
        ],
        compiler_params=pltpu.CompilerParams(vmem_limit_bytes=56 * 2**20),
        name="attend",
    )(feat_pad, cot, gain, w_t, wo)


def back_kernel(factor, feat, cot, dq, dkv, att, gain, w_t, w_all, grad_out, sums_out):
    cols, chans = feat.shape[1], feat.shape[2]
    step = pl.program_id(0)

    @pl.when(step == 0)
    def _():
        sums_out[...] = jnp.zeros_like(sums_out)

    x = lanes(feat, 0, range(cols)).astype(f32)
    normed, scaled, inv = normalized(x, gain[...])
    raw = matmul(w_t[...], normed)

    def unit_back(part, grad):
        part_inv = unit_inv(part)
        unit = part * part_inv
        return part_inv * (grad - unit * jnp.mean(grad * unit, axis=0, keepdims=True))

    d_kv = lanes(dkv, 0, range(cols)).astype(f32)
    d_query = unit_back(raw[:chans], lanes(dq, 0, range(cols)).astype(f32))
    d_key = unit_back(raw[chans : 2 * chans], d_kv[:chans])
    raw_grad = jnp.concatenate([d_query, d_key, d_kv[chans:]], axis=0).astype(bf16)
    normed_grad = matmul(w_all[...], raw_grad)
    m = normed_grad * gain[...]
    cot_block = lanes(cot, 0, range(cols))
    branch = inv * (m - scaled * jnp.mean(m * scaled, axis=0, keepdims=True))
    out = (cot_block.astype(f32) + branch).astype(bf16)
    pix = feat.shape[3]
    for c in range(cols):
        grad_out[0, c] = out[:, c * pix : (c + 1) * pix]
    weight = jnp.concatenate(
        [matmul_nt(normed, raw_grad), matmul_nt(lanes(att, 0, range(cols)), cot_block)], axis=1
    )
    sums_out[:chans, :] += weight * factor
    ones = jnp.ones((8, cols * pix), bf16)
    sums_out[chans:, :chans] += matmul_nt(ones, (normed_grad * scaled).astype(bf16)) * factor


def back(factor, feat, cot, dq, dkv, att, gain, w_t, w_all):
    rows, cols, chans, pix = feat.shape

    def by_row(width):
        return pl.BlockSpec((1, cols, width, pix), lambda r: (r, 0, 0, 0))

    def fixed(array):
        return pl.BlockSpec(array.shape, lambda r: (0, 0))

    sums = jax.ShapeDtypeStruct((chans + 8, 4 * chans), f32)
    return pl.pallas_call(
        functools.partial(back_kernel, factor),
        grid=(rows,),
        out_shape=(jax.ShapeDtypeStruct(feat.shape, bf16), sums),
        in_specs=[by_row(chans), by_row(chans), by_row(chans), by_row(2 * chans), by_row(chans)]
        + [fixed(gain), fixed(w_t), fixed(w_all)],
        out_specs=(by_row(chans), fixed(sums)),
        compiler_params=pltpu.CompilerParams(vmem_limit_bytes=32 * 2**20),
        name="back",
    )(feat, cot, dq, dkv, att, gain, w_t, w_all)


def extended(block, axis, dim):
    length = block.shape[dim]
    before = shift(lax.slice_in_dim(block, length - REACH, length, axis=dim), axis, True)
    after = shift(lax.slice_in_dim(block, 0, REACH, axis=dim), axis, False)
    return jnp.concatenate([before, block, after], axis=dim)


def folded(block, axis, dim):
    length = block.shape[dim]
    to_before = lax.slice_in_dim(block, 0, REACH, axis=dim)
    to_after = lax.slice_in_dim(block, length - REACH, length, axis=dim)
    from_after = shift(to_before, axis, False)
    from_before = shift(to_after, axis, True)
    own = lax.slice_in_dim(block, REACH, length - REACH, axis=dim)
    first = (slice(None),) * dim + (slice(0, REACH),)
    last = (slice(None),) * dim + (slice(own.shape[dim] - REACH, None),)
    return own.at[first].add(from_before).at[last].add(from_after)


def body(features, out_cotangent, norm_gain, query_proj, keyval_proj, output_proj):
    gain = norm_gain[:, None]
    w_all = jnp.concatenate([query_proj, keyval_proj], axis=1)
    w_t = w_all.T
    feat_pad = extended(extended(features, "vrow", 0), "vcol", 1)
    dq, att, dkv = attend(feat_pad, out_cotangent, gain, w_t, output_proj)
    dkv = folded(folded(dkv, "vcol", 1), "vrow", 0)
    rows, cols, chans, pix = features.shape
    axes = ("vrow", "vcol", "pix")
    tokens_all = rows * cols * pix * math.prod(lax.axis_size(a) for a in axes)
    grad, sums = back(
        tokens_all**-0.5, features, out_cotangent, dq, dkv, att, gain, w_t, w_all
    )
    sums = lax.psum(sums, axes)
    return (
        grad,
        sums[:chans, :chans],
        sums[:chans, chans : 3 * chans],
        sums[:chans, 3 * chans :],
        sums[chans, :chans],
    )


def solution(mesh):
    placed = P("vrow", "vcol", None, "pix")
    return jax.shard_map(
        body,
        mesh=mesh,
        in_specs=(placed, placed, P(), P(), P(), P()),
        out_specs=(placed, P(), P(), P(), P()),
        check_vma=False,
    )
```

```python
import functools
import math

import jax
import jax.numpy as jnp
from jax import lax
from jax.experimental import pallas as pl
from jax.experimental.pallas import tpu as pltpu
from jax.sharding import PartitionSpec as P

HEADS = 4
REACH = 2
SPAN = 2 * REACH + 1
EPSILON = 1e-06
f32, bf16 = jnp.float32, jnp.bfloat16


def shift(block, axis, up):
    count = lax.axis_size(axis)
    pairs = [(i, i + 1) if up else (i + 1, i) for i in range(count - 1)]
    return lax.ppermute(block, axis, pairs)


def lanes(ref, row, cols):
    return jnp.concatenate([ref[row, c] for c in cols], axis=1)


def unit_inv(raw):
    return lax.rsqrt(jnp.mean(raw * raw, axis=0, keepdims=True) + EPSILON)


def matmul(a, b):
    return jnp.dot(a, b, preferred_element_type=f32)


def matmul_nt(a, b):
    return lax.dot_general(a, b, (((1,), (1,)), ((), ())), preferred_element_type=f32)


def normalized(x, gain):
    inv = lax.rsqrt(jnp.mean(x * x, axis=0, keepdims=True) + EPSILON)
    scaled = x * inv
    return (scaled * gain).astype(bf16), scaled, inv


def attend_kernel(
    feat, cot, gain, w_t, wo, dq_out, att_out, dkv_out, q_s, g_s, kv_s, dkv_s, w_s, dp_s, dq_s, att_s
):
    rows, cols, chans, pix = cot.shape
    rows_p, cols_p = feat.shape[:2]
    size = chans // HEADS
    scale = size ** (-0.5)
    kv_row = 2 * chans * cols_p
    q_row = chans * cols
    own = range(REACH, REACH + cols)

    def front(row, _):
        x = lanes(feat, row, range(cols_p)).astype(f32)
        normed, _, _ = normalized(x, gain[...])
        raw = matmul(w_t[...], normed)
        raw_q, raw_k, value = raw[:chans], raw[chans : 2 * chans], raw[2 * chans :]
        query = (raw_q * unit_inv(raw_q)).astype(bf16).astype(f32)
        key = (raw_k * unit_inv(raw_k)).astype(bf16).astype(f32)
        value = value.astype(bf16).astype(f32)
        for c in range(cols_p):
            at = slice(c * pix, (c + 1) * pix)
            kv_s[pl.ds(row * kv_row + c, chans, stride=cols_p), :] = key[:, at]
            kv_s[pl.ds(row * kv_row + chans * cols_p + c, chans, stride=cols_p), :] = value[:, at]
        for i, c in enumerate(own):
            q_s[pl.ds(row * q_row + i, chans, stride=cols), :] = query[:, c * pix : (c + 1) * pix]
        dkv_s[pl.ds(row * kv_row, kv_row), :] = jnp.zeros((kv_row, pix), f32)
        return 0

    lax.fori_loop(0, rows_p, front, 0)

    def grads(row, _):
        out_grad = matmul(wo[...], lanes(cot, row, range(cols)))
        for i in range(cols):
            g_s[pl.ds(row * q_row + i, chans, stride=cols), :] = out_grad[:, i * pix : (i + 1) * pix]
        return 0

    lax.fori_loop(0, rows, grads, 0)

    def one(step, _):
        row, head = step // HEADS, step % HEADS
        q_at = (row + REACH) * q_row + head * size * cols
        g_at = row * q_row + head * size * cols
        q = [q_s[pl.ds(q_at + c * cols, cols), :] for c in range(size)]
        g = [g_s[pl.ds(g_at + c * cols, cols), :] for c in range(size)]
        v_off = chans * cols_p

        def fold(parts):
            while len(parts) > 1:
                parts = [a + b for a, b in zip(parts[::2], parts[1::2])]
            return parts[0]

        def forward(a, carry):
            total, w_dp, att = carry
            base = (row + a) * kv_row + head * size * cols_p
            for b in range(SPAN):
                def k(c):
                    return kv_s[pl.ds(base + (b + c * cols_p), cols), :]

                def v(c):
                    return kv_s[pl.ds(base + (v_off + b + c * cols_p), cols), :]

                w = jnp.exp(fold([q[c] * k(c) for c in range(size)]) * scale)
                dp = fold([g[c] * v(c) for c in range(size)])
                att = [att[c] + w * v(c) for c in range(size)]
                total = total + w
                w_dp = w_dp + w * dp
                at = pl.ds((a * SPAN + b) * cols, cols)
                w_s[at, :] = w
                dp_s[at, :] = dp
            return total, w_dp, att

        zero = jnp.zeros((cols, pix), f32)
        total, w_dp, att = lax.fori_loop(0, SPAN, forward, (zero, zero, [zero] * size))
        inv = 1.0 / total
        spread = w_dp * inv
        for c in range(size):
            att_s[pl.ds(g_at + c * cols, cols), :] = att[c] * inv

        def back(a, dq):
            base = (row + a) * kv_row + head * size * cols_p
            for b in range(SPAN):
                at = pl.ds((a * SPAN + b) * cols, cols)
                p = w_s[at, :] * inv
                ds = p * (dp_s[at, :] - spread) * scale
                dq = [dq[c] + ds * kv_s[pl.ds(base + (b + c * cols_p), cols), :] for c in range(size)]
                for c in range(size):
                    dkv_s[pl.ds(base + (b + c * cols_p), cols), :] += ds * q[c]
                for c in range(size):
                    dkv_s[pl.ds(base + (v_off + b + c * cols_p), cols), :] += p * g[c]
            return dq

        dq = lax.fori_loop(0, SPAN, back, [zero] * size)
        for c in range(size):
            dq_s[pl.ds(g_at + c * cols, cols), :] = dq[c]
        return 0

    lax.fori_loop(0, rows * HEADS, one, 0)

    def finish(row, _):
        for i in range(cols):
            dq_out[row, i] = dq_s[pl.ds(row * q_row + i, chans, stride=cols), :].astype(bf16)
            att_out[row, i] = att_s[pl.ds(row * q_row + i, chans, stride=cols), :].astype(bf16)
        return 0

    lax.fori_loop(0, rows, finish, 0)

    def finish_kv(row, _):
        for c in range(cols_p):
            dkv_out[row, c] = dkv_s[pl.ds(row * kv_row + c, 2 * chans, stride=cols_p), :].astype(bf16)
        return 0

    lax.fori_loop(0, rows_p, finish_kv, 0)


def attend(feat_pad, cot, gain, w_t, wo):
    rows, cols, chans, pix = cot.shape
    rows_p, cols_p = feat_pad.shape[:2]
    own = rows * chans * cols
    pad_kv = rows_p * 2 * chans * cols_p
    whole = pl.BlockSpec(memory_space=pltpu.VMEM)
    return pl.pallas_call(
        attend_kernel,
        out_shape=(
            jax.ShapeDtypeStruct(cot.shape, bf16),
            jax.ShapeDtypeStruct(cot.shape, bf16),
            jax.ShapeDtypeStruct((rows_p, cols_p, 2 * chans, pix), bf16),
        ),
        in_specs=[whole] * 5,
        out_specs=(whole,) * 3,
        scratch_shapes=[
            pltpu.VMEM((rows_p * chans * cols, pix), f32),
            pltpu.VMEM((own, pix), f32),
            pltpu.VMEM((pad_kv, pix), f32),
            pltpu.VMEM((pad_kv, pix), f32),
            pltpu.VMEM((SPAN * SPAN * cols, pix), f32),
            pltpu.VMEM((SPAN * SPAN * cols, pix), f32),
            pltpu.VMEM((own, pix), f32),
            pltpu.VMEM((own, pix), f32),
        ],
        compiler_params=pltpu.CompilerParams(vmem_limit_bytes=56 * 2**20),
        name="attend",
    )(feat_pad, cot, gain, w_t, wo)


def back_kernel(factor, feat, cot, dq, dkv, att, gain, w_t, w_all, grad_out, sums_out):
    cols, chans = feat.shape[1], feat.shape[2]
    step = pl.program_id(0)

    @pl.when(step == 0)
    def _():
        sums_out[...] = jnp.zeros_like(sums_out)

    x = lanes(feat, 0, range(cols)).astype(f32)
    normed, scaled, inv = normalized(x, gain[...])
    raw = matmul(w_t[...], normed)

    def unit_back(part, grad):
        part_inv = unit_inv(part)
        unit = part * part_inv
        return part_inv * (grad - unit * jnp.mean(grad * unit, axis=0, keepdims=True))

    d_kv = lanes(dkv, 0, range(cols)).astype(f32)
    d_query = unit_back(raw[:chans], lanes(dq, 0, range(cols)).astype(f32))
    d_key = unit_back(raw[chans : 2 * chans], d_kv[:chans])
    raw_grad = jnp.concatenate([d_query, d_key, d_kv[chans:]], axis=0).astype(bf16)
    normed_grad = matmul(w_all[...], raw_grad)
    m = normed_grad * gain[...]
    cot_block = lanes(cot, 0, range(cols))
    branch = inv * (m - scaled * jnp.mean(m * scaled, axis=0, keepdims=True))
    out = (cot_block.astype(f32) + branch).astype(bf16)
    pix = feat.shape[3]
    for c in range(cols):
        grad_out[0, c] = out[:, c * pix : (c + 1) * pix]
    weight = jnp.concatenate(
        [matmul_nt(normed, raw_grad), matmul_nt(lanes(att, 0, range(cols)), cot_block)], axis=1
    )
    sums_out[:chans, :] += weight * factor
    ones = jnp.ones((8, cols * pix), bf16)
    sums_out[chans:, :chans] += matmul_nt(ones, (normed_grad * scaled).astype(bf16)) * factor


def back(factor, feat, cot, dq, dkv, att, gain, w_t, w_all):
    rows, cols, chans, pix = feat.shape

    def by_row(width):
        return pl.BlockSpec((1, cols, width, pix), lambda r: (r, 0, 0, 0))

    def fixed(array):
        return pl.BlockSpec(array.shape, lambda r: (0, 0))

    sums = jax.ShapeDtypeStruct((chans + 8, 4 * chans), f32)
    return pl.pallas_call(
        functools.partial(back_kernel, factor),
        grid=(rows,),
        out_shape=(jax.ShapeDtypeStruct(feat.shape, bf16), sums),
        in_specs=[by_row(chans), by_row(chans), by_row(chans), by_row(2 * chans), by_row(chans)]
        + [fixed(gain), fixed(w_t), fixed(w_all)],
        out_specs=(by_row(chans), fixed(sums)),
        compiler_params=pltpu.CompilerParams(vmem_limit_bytes=32 * 2**20),
        name="back",
    )(feat, cot, dq, dkv, att, gain, w_t, w_all)


def summed(block, axes):
    for axis in axes:
        count = lax.axis_size(axis)
        if count & (count - 1):
            block = lax.psum(block, axis)
            continue
        hop = 1
        while hop < count:
            block = block + lax.ppermute(block, axis, [(i, i ^ hop) for i in range(count)])
            hop *= 2
    return block


def extended(block, axis, dim):
    length = block.shape[dim]
    before = shift(lax.slice_in_dim(block, length - REACH, length, axis=dim), axis, True)
    after = shift(lax.slice_in_dim(block, 0, REACH, axis=dim), axis, False)
    return jnp.concatenate([before, block, after], axis=dim)


def folded(block, axis, dim):
    length = block.shape[dim]
    to_before = lax.slice_in_dim(block, 0, REACH, axis=dim)
    to_after = lax.slice_in_dim(block, length - REACH, length, axis=dim)
    from_after = shift(to_before, axis, False)
    from_before = shift(to_after, axis, True)
    own = lax.slice_in_dim(block, REACH, length - REACH, axis=dim)
    first = (slice(None),) * dim + (slice(0, REACH),)
    last = (slice(None),) * dim + (slice(own.shape[dim] - REACH, None),)
    return own.at[first].add(from_before).at[last].add(from_after)


def body(features, out_cotangent, norm_gain, query_proj, keyval_proj, output_proj):
    gain = norm_gain[:, None]
    w_all = jnp.concatenate([query_proj, keyval_proj], axis=1)
    w_t = w_all.T
    feat_pad = extended(extended(features, "vrow", 0), "vcol", 1)
    dq, att, dkv = attend(feat_pad, out_cotangent, gain, w_t, output_proj)
    dkv = folded(folded(dkv, "vcol", 1), "vrow", 0)
    rows, cols, chans, pix = features.shape
    axes = ("vrow", "vcol", "pix")
    tokens_all = rows * cols * pix * math.prod(lax.axis_size(a) for a in axes)
    grad, sums = back(
        tokens_all**-0.5, features, out_cotangent, dq, dkv, att, gain, w_t, w_all
    )
    sums = summed(sums, axes[::-1])
    return (
        grad,
        sums[:chans, :chans],
        sums[:chans, chans : 3 * chans],
        sums[:chans, 3 * chans :],
        sums[chans, :chans],
    )


def solution(mesh):
    placed = P("vrow", "vcol", None, "pix")
    return jax.shard_map(
        body,
        mesh=mesh,
        in_specs=(placed, placed, P(), P(), P(), P()),
        out_specs=(placed, P(), P(), P(), P()),
        check_vma=False,
    )
```

```python
import functools
import math

import jax
import jax.numpy as jnp
from jax import lax
from jax.experimental import pallas as pl
from jax.experimental.pallas import tpu as pltpu
from jax.sharding import PartitionSpec as P

HEADS = 4
REACH = 2
SPAN = 2 * REACH + 1
EPSILON = 1e-06
f32, bf16 = jnp.float32, jnp.bfloat16


def shift(block, axis, up):
    count = lax.axis_size(axis)
    pairs = [(i, i + 1) if up else (i + 1, i) for i in range(count - 1)]
    return lax.ppermute(block, axis, pairs)


def exchange(to_before, to_after, axis):
    if lax.axis_size(axis) != 2:
        return shift(to_after, axis, True), shift(to_before, axis, False)
    first = lax.axis_index(axis) == 0
    came = lax.ppermute(jnp.where(first, to_after, to_before), axis, [(0, 1), (1, 0)])
    none = jnp.zeros_like(came)
    return jnp.where(first, none, came), jnp.where(first, came, none)


def lanes(ref, row, cols):
    return jnp.concatenate([ref[row, c] for c in cols], axis=1)


def unit_inv(raw):
    return lax.rsqrt(jnp.mean(raw * raw, axis=0, keepdims=True) + EPSILON)


def matmul(a, b):
    return jnp.dot(a, b, preferred_element_type=f32)


def matmul_nt(a, b):
    return lax.dot_general(a, b, (((1,), (1,)), ((), ())), preferred_element_type=f32)


def normalized(x, gain):
    inv = lax.rsqrt(jnp.mean(x * x, axis=0, keepdims=True) + EPSILON)
    scaled = x * inv
    return (scaled * gain).astype(bf16), scaled, inv


def attend_kernel(
    feat, cot, gain, w_t, wo, dq_out, att_out, dkv_out, q_s, g_s, kv_s, dkv_s, w_s, dp_s, dq_s, att_s
):
    rows, cols, chans, pix = cot.shape
    rows_p, cols_p = feat.shape[:2]
    size = chans // HEADS
    scale = size ** (-0.5)
    kv_row = 2 * chans * cols_p
    q_row = chans * cols
    own = range(REACH, REACH + cols)

    def front(row, _):
        x = lanes(feat, row, range(cols_p)).astype(f32)
        normed, _, _ = normalized(x, gain[...])
        raw = matmul(w_t[...], normed)
        raw_q, raw_k, value = raw[:chans], raw[chans : 2 * chans], raw[2 * chans :]
        query = (raw_q * unit_inv(raw_q)).astype(bf16).astype(f32)
        key = (raw_k * unit_inv(raw_k)).astype(bf16).astype(f32)
        value = value.astype(bf16).astype(f32)
        for c in range(cols_p):
            at = slice(c * pix, (c + 1) * pix)
            kv_s[pl.ds(row * kv_row + c, chans, stride=cols_p), :] = key[:, at]
            kv_s[pl.ds(row * kv_row + chans * cols_p + c, chans, stride=cols_p), :] = value[:, at]
        for i, c in enumerate(own):
            q_s[pl.ds(row * q_row + i, chans, stride=cols), :] = query[:, c * pix : (c + 1) * pix]
        dkv_s[pl.ds(row * kv_row, kv_row), :] = jnp.zeros((kv_row, pix), f32)
        return 0

    lax.fori_loop(0, rows_p, front, 0)

    def grads(row, _):
        out_grad = matmul(wo[...], lanes(cot, row, range(cols)))
        for i in range(cols):
            g_s[pl.ds(row * q_row + i, chans, stride=cols), :] = out_grad[:, i * pix : (i + 1) * pix]
        return 0

    lax.fori_loop(0, rows, grads, 0)

    def one(step, _):
        row, head = step // HEADS, step % HEADS
        q_at = (row + REACH) * q_row + head * size * cols
        g_at = row * q_row + head * size * cols
        q = [q_s[pl.ds(q_at + c * cols, cols), :] for c in range(size)]
        g = [g_s[pl.ds(g_at + c * cols, cols), :] for c in range(size)]
        v_off = chans * cols_p

        def fold(parts):
            while len(parts) > 1:
                parts = [a + b for a, b in zip(parts[::2], parts[1::2])]
            return parts[0]

        def forward(a, carry):
            total, w_dp, att = carry
            base = (row + a) * kv_row + head * size * cols_p
            for b in range(SPAN):
                def k(c):
                    return kv_s[pl.ds(base + (b + c * cols_p), cols), :]

                def v(c):
                    return kv_s[pl.ds(base + (v_off + b + c * cols_p), cols), :]

                w = jnp.exp(fold([q[c] * k(c) for c in range(size)]) * scale)
                dp = fold([g[c] * v(c) for c in range(size)])
                att = [att[c] + w * v(c) for c in range(size)]
                total = total + w
                w_dp = w_dp + w * dp
                at = pl.ds((a * SPAN + b) * cols, cols)
                w_s[at, :] = w
                dp_s[at, :] = dp
            return total, w_dp, att

        zero = jnp.zeros((cols, pix), f32)
        total, w_dp, att = lax.fori_loop(0, SPAN, forward, (zero, zero, [zero] * size))
        inv = 1.0 / total
        spread = w_dp * inv
        for c in range(size):
            att_s[pl.ds(g_at + c * cols, cols), :] = att[c] * inv

        def back(a, dq):
            base = (row + a) * kv_row + head * size * cols_p
            for b in range(SPAN):
                at = pl.ds((a * SPAN + b) * cols, cols)
                p = w_s[at, :] * inv
                ds = p * (dp_s[at, :] - spread) * scale
                dq = [dq[c] + ds * kv_s[pl.ds(base + (b + c * cols_p), cols), :] for c in range(size)]
                for c in range(size):
                    dkv_s[pl.ds(base + (b + c * cols_p), cols), :] += ds * q[c]
                for c in range(size):
                    dkv_s[pl.ds(base + (v_off + b + c * cols_p), cols), :] += p * g[c]
            return dq

        dq = lax.fori_loop(0, SPAN, back, [zero] * size)
        for c in range(size):
            dq_s[pl.ds(g_at + c * cols, cols), :] = dq[c]
        return 0

    lax.fori_loop(0, rows * HEADS, one, 0)

    def finish(row, _):
        for i in range(cols):
            dq_out[row, i] = dq_s[pl.ds(row * q_row + i, chans, stride=cols), :].astype(bf16)
            att_out[row, i] = att_s[pl.ds(row * q_row + i, chans, stride=cols), :].astype(bf16)
        return 0

    lax.fori_loop(0, rows, finish, 0)

    def finish_kv(row, _):
        for c in range(cols_p):
            dkv_out[row, c] = dkv_s[pl.ds(row * kv_row + c, 2 * chans, stride=cols_p), :].astype(bf16)
        return 0

    lax.fori_loop(0, rows_p, finish_kv, 0)


def attend(feat_pad, cot, gain, w_t, wo):
    rows, cols, chans, pix = cot.shape
    rows_p, cols_p = feat_pad.shape[:2]
    own = rows * chans * cols
    pad_kv = rows_p * 2 * chans * cols_p
    whole = pl.BlockSpec(memory_space=pltpu.VMEM)
    return pl.pallas_call(
        attend_kernel,
        out_shape=(
            jax.ShapeDtypeStruct(cot.shape, bf16),
            jax.ShapeDtypeStruct(cot.shape, bf16),
            jax.ShapeDtypeStruct((rows_p, cols_p, 2 * chans, pix), bf16),
        ),
        in_specs=[whole] * 5,
        out_specs=(whole,) * 3,
        scratch_shapes=[
            pltpu.VMEM((rows_p * chans * cols, pix), f32),
            pltpu.VMEM((own, pix), f32),
            pltpu.VMEM((pad_kv, pix), f32),
            pltpu.VMEM((pad_kv, pix), f32),
            pltpu.VMEM((SPAN * SPAN * cols, pix), f32),
            pltpu.VMEM((SPAN * SPAN * cols, pix), f32),
            pltpu.VMEM((own, pix), f32),
            pltpu.VMEM((own, pix), f32),
        ],
        compiler_params=pltpu.CompilerParams(vmem_limit_bytes=56 * 2**20),
        name="attend",
    )(feat_pad, cot, gain, w_t, wo)


def back_kernel(factor, feat, cot, dq, dkv, att, gain, w_t, w_all, grad_out, sums_out):
    cols, chans = feat.shape[1], feat.shape[2]
    step = pl.program_id(0)

    @pl.when(step == 0)
    def _():
        sums_out[...] = jnp.zeros_like(sums_out)

    x = lanes(feat, 0, range(cols)).astype(f32)
    normed, scaled, inv = normalized(x, gain[...])
    raw = matmul(w_t[...], normed)

    def unit_back(part, grad):
        part_inv = unit_inv(part)
        unit = part * part_inv
        return part_inv * (grad - unit * jnp.mean(grad * unit, axis=0, keepdims=True))

    d_kv = lanes(dkv, 0, range(cols)).astype(f32)
    d_query = unit_back(raw[:chans], lanes(dq, 0, range(cols)).astype(f32))
    d_key = unit_back(raw[chans : 2 * chans], d_kv[:chans])
    raw_grad = jnp.concatenate([d_query, d_key, d_kv[chans:]], axis=0).astype(bf16)
    normed_grad = matmul(w_all[...], raw_grad)
    m = normed_grad * gain[...]
    cot_block = lanes(cot, 0, range(cols))
    branch = inv * (m - scaled * jnp.mean(m * scaled, axis=0, keepdims=True))
    out = (cot_block.astype(f32) + branch).astype(bf16)
    pix = feat.shape[3]
    for c in range(cols):
        grad_out[0, c] = out[:, c * pix : (c + 1) * pix]
    weight = jnp.concatenate(
        [matmul_nt(normed, raw_grad), matmul_nt(lanes(att, 0, range(cols)), cot_block)], axis=1
    )
    sums_out[:chans, :] += weight * factor
    ones = jnp.ones((8, cols * pix), bf16)
    sums_out[chans:, :chans] += matmul_nt(ones, (normed_grad * scaled).astype(bf16)) * factor


def back(factor, feat, cot, dq, dkv, att, gain, w_t, w_all):
    rows, cols, chans, pix = feat.shape

    def by_row(width):
        return pl.BlockSpec((1, cols, width, pix), lambda r: (r, 0, 0, 0))

    def fixed(array):
        return pl.BlockSpec(array.shape, lambda r: (0, 0))

    sums = jax.ShapeDtypeStruct((chans + 8, 4 * chans), f32)
    return pl.pallas_call(
        functools.partial(back_kernel, factor),
        grid=(rows,),
        out_shape=(jax.ShapeDtypeStruct(feat.shape, bf16), sums),
        in_specs=[by_row(chans), by_row(chans), by_row(chans), by_row(2 * chans), by_row(chans)]
        + [fixed(gain), fixed(w_t), fixed(w_all)],
        out_specs=(by_row(chans), fixed(sums)),
        compiler_params=pltpu.CompilerParams(vmem_limit_bytes=32 * 2**20),
        name="back",
    )(feat, cot, dq, dkv, att, gain, w_t, w_all)


def summed(block, axes):
    for axis in axes:
        count = lax.axis_size(axis)
        if count & (count - 1):
            block = lax.psum(block, axis)
            continue
        hop = 1
        while hop < count:
            block = block + lax.ppermute(block, axis, [(i, i ^ hop) for i in range(count)])
            hop *= 2
    return block


def extended(block, axis, dim):
    length = block.shape[dim]
    leading = lax.slice_in_dim(block, 0, REACH, axis=dim)
    last = lax.slice_in_dim(block, length - REACH, length, axis=dim)
    before, after = exchange(leading, last, axis)
    return jnp.concatenate([before, block, after], axis=dim)


def folded(block, axis, dim):
    length = block.shape[dim]
    to_before = lax.slice_in_dim(block, 0, REACH, axis=dim)
    to_after = lax.slice_in_dim(block, length - REACH, length, axis=dim)
    from_before, from_after = exchange(to_before, to_after, axis)
    own = lax.slice_in_dim(block, REACH, length - REACH, axis=dim)
    first = (slice(None),) * dim + (slice(0, REACH),)
    last = (slice(None),) * dim + (slice(own.shape[dim] - REACH, None),)
    return own.at[first].add(from_before).at[last].add(from_after)


def body(features, out_cotangent, norm_gain, query_proj, keyval_proj, output_proj):
    gain = norm_gain[:, None]
    w_all = jnp.concatenate([query_proj, keyval_proj], axis=1)
    w_t = w_all.T
    feat_pad = extended(extended(features, "vrow", 0), "vcol", 1)
    dq, att, dkv = attend(feat_pad, out_cotangent, gain, w_t, output_proj)
    dkv = folded(folded(dkv, "vcol", 1), "vrow", 0)
    rows, cols, chans, pix = features.shape
    axes = ("vrow", "vcol", "pix")
    tokens_all = rows * cols * pix * math.prod(lax.axis_size(a) for a in axes)
    grad, sums = back(
        tokens_all**-0.5, features, out_cotangent, dq, dkv, att, gain, w_t, w_all
    )
    sums = summed(sums, axes[::-1])
    return (
        grad,
        sums[:chans, :chans],
        sums[:chans, chans : 3 * chans],
        sums[:chans, 3 * chans :],
        sums[chans, :chans],
    )


def solution(mesh):
    placed = P("vrow", "vcol", None, "pix")
    return jax.shard_map(
        body,
        mesh=mesh,
        in_specs=(placed, placed, P(), P(), P(), P()),
        out_specs=(placed, P(), P(), P(), P()),
        check_vma=False,
    )
```

```python
import functools
import math

import jax
import jax.numpy as jnp
from jax import lax
from jax.experimental import pallas as pl
from jax.experimental.pallas import tpu as pltpu
from jax.sharding import PartitionSpec as P

HEADS = 4
REACH = 2
SPAN = 2 * REACH + 1
EPSILON = 1e-06
f32, bf16 = jnp.float32, jnp.bfloat16


def shift(block, axis, up):
    count = lax.axis_size(axis)
    pairs = [(i, i + 1) if up else (i + 1, i) for i in range(count - 1)]
    return lax.ppermute(block, axis, pairs)


def exchange(to_before, to_after, axis):
    if lax.axis_size(axis) != 2:
        return shift(to_after, axis, True), shift(to_before, axis, False)
    first = lax.axis_index(axis) == 0
    came = lax.ppermute(jnp.where(first, to_after, to_before), axis, [(0, 1), (1, 0)])
    none = jnp.zeros_like(came)
    return jnp.where(first, none, came), jnp.where(first, came, none)


def lanes(ref, row, cols):
    return jnp.concatenate([ref[row, c] for c in cols], axis=1)


def unit_inv(raw):
    return lax.rsqrt(jnp.mean(raw * raw, axis=0, keepdims=True) + EPSILON)


def matmul(a, b):
    return jnp.dot(a, b, preferred_element_type=f32)


def matmul_nt(a, b):
    return lax.dot_general(a, b, (((1,), (1,)), ((), ())), preferred_element_type=f32)


def normalized(x, gain):
    inv = lax.rsqrt(jnp.mean(x * x, axis=0, keepdims=True) + EPSILON)
    scaled = x * inv
    return (scaled * gain).astype(bf16), scaled, inv


def attend_kernel(
    feat, cot, gain, w_t, wo, dq_out, att_out, dkv_out, q_s, g_s, kv_s, dkv_s, w_s, dp_s, dq_s, att_s
):
    rows, cols, chans, pix = cot.shape
    rows_p, cols_p = feat.shape[:2]
    size = chans // HEADS
    scale = size ** (-0.5)
    kv_row = 2 * chans * cols_p
    q_row = chans * cols
    own = range(REACH, REACH + cols)

    def front(row, _):
        x = lanes(feat, row, range(cols_p)).astype(f32)
        normed, _, _ = normalized(x, gain[...])
        raw = matmul(w_t[...], normed)
        raw_q, raw_k, value = raw[:chans], raw[chans : 2 * chans], raw[2 * chans :]
        query = (raw_q * unit_inv(raw_q)).astype(bf16).astype(f32)
        key = (raw_k * unit_inv(raw_k)).astype(bf16).astype(f32)
        value = value.astype(bf16).astype(f32)
        for c in range(cols_p):
            at = slice(c * pix, (c + 1) * pix)
            kv_s[pl.ds(row * kv_row + c, chans, stride=cols_p), :] = key[:, at]
            kv_s[pl.ds(row * kv_row + chans * cols_p + c, chans, stride=cols_p), :] = value[:, at]
        for i, c in enumerate(own):
            q_s[pl.ds(row * q_row + i, chans, stride=cols), :] = query[:, c * pix : (c + 1) * pix]
        dkv_s[pl.ds(row * kv_row, kv_row), :] = jnp.zeros((kv_row, pix), f32)
        return 0

    lax.fori_loop(0, rows_p, front, 0)

    def grads(row, _):
        out_grad = matmul(wo[...], lanes(cot, row, range(cols)))
        for i in range(cols):
            g_s[pl.ds(row * q_row + i, chans, stride=cols), :] = out_grad[:, i * pix : (i + 1) * pix]
        return 0

    lax.fori_loop(0, rows, grads, 0)

    def one(step, _):
        row, head = step // HEADS, step % HEADS
        q_at = (row + REACH) * q_row + head * size * cols
        g_at = row * q_row + head * size * cols
        q = [q_s[pl.ds(q_at + c * cols, cols), :] for c in range(size)]
        g = [g_s[pl.ds(g_at + c * cols, cols), :] for c in range(size)]
        v_off = chans * cols_p

        def fold(parts):
            while len(parts) > 1:
                parts = [a + b for a, b in zip(parts[::2], parts[1::2])]
            return parts[0]

        def forward(a, carry):
            total, w_dp, att = carry
            base = (row + a) * kv_row + head * size * cols_p
            for b in range(SPAN):
                def k(c):
                    return kv_s[pl.ds(base + (b + c * cols_p), cols), :]

                def v(c):
                    return kv_s[pl.ds(base + (v_off + b + c * cols_p), cols), :]

                w = jnp.exp(fold([q[c] * k(c) for c in range(size)]) * scale)
                dp = fold([g[c] * v(c) for c in range(size)])
                att = [att[c] + w * v(c) for c in range(size)]
                total = total + w
                w_dp = w_dp + w * dp
                at = pl.ds((a * SPAN + b) * cols, cols)
                w_s[at, :] = w
                dp_s[at, :] = dp
            return total, w_dp, att

        zero = jnp.zeros((cols, pix), f32)
        total, w_dp, att = lax.fori_loop(0, SPAN, forward, (zero, zero, [zero] * size))
        inv = 1.0 / total
        spread = w_dp * inv
        for c in range(size):
            att_s[pl.ds(g_at + c * cols, cols), :] = att[c] * inv

        def back(a, dq):
            base = (row + a) * kv_row + head * size * cols_p
            for b in range(SPAN):
                at = pl.ds((a * SPAN + b) * cols, cols)
                p = w_s[at, :] * inv
                ds = p * (dp_s[at, :] - spread) * scale
                dq = [dq[c] + ds * kv_s[pl.ds(base + (b + c * cols_p), cols), :] for c in range(size)]
                for c in range(size):
                    dkv_s[pl.ds(base + (b + c * cols_p), cols), :] += ds * q[c]
                for c in range(size):
                    dkv_s[pl.ds(base + (v_off + b + c * cols_p), cols), :] += p * g[c]
            return dq

        dq = lax.fori_loop(0, SPAN, back, [zero] * size)
        for c in range(size):
            dq_s[pl.ds(g_at + c * cols, cols), :] = dq[c]
        return 0

    lax.fori_loop(0, rows * HEADS, one, 0)

    def finish(row, _):
        for i in range(cols):
            dq_out[row, i] = dq_s[pl.ds(row * q_row + i, chans, stride=cols), :].astype(bf16)
            att_out[row, i] = att_s[pl.ds(row * q_row + i, chans, stride=cols), :].astype(bf16)
        return 0

    lax.fori_loop(0, rows, finish, 0)

    def finish_kv(row, _):
        for c in range(cols_p):
            dkv_out[row, c] = dkv_s[pl.ds(row * kv_row + c, 2 * chans, stride=cols_p), :].astype(bf16)
        return 0

    lax.fori_loop(0, rows_p, finish_kv, 0)


def attend(feat_pad, cot, gain, w_t, wo):
    rows, cols, chans, pix = cot.shape
    rows_p, cols_p = feat_pad.shape[:2]
    own = rows * chans * cols
    pad_kv = rows_p * 2 * chans * cols_p
    whole = pl.BlockSpec(memory_space=pltpu.VMEM)
    return pl.pallas_call(
        attend_kernel,
        out_shape=(
            jax.ShapeDtypeStruct(cot.shape, bf16),
            jax.ShapeDtypeStruct(cot.shape, bf16),
            jax.ShapeDtypeStruct((rows_p, cols_p, 2 * chans, pix), bf16),
        ),
        in_specs=[whole] * 5,
        out_specs=(whole,) * 3,
        scratch_shapes=[
            pltpu.VMEM((rows_p * chans * cols, pix), f32),
            pltpu.VMEM((own, pix), f32),
            pltpu.VMEM((pad_kv, pix), f32),
            pltpu.VMEM((pad_kv, pix), f32),
            pltpu.VMEM((SPAN * SPAN * cols, pix), f32),
            pltpu.VMEM((SPAN * SPAN * cols, pix), f32),
            pltpu.VMEM((own, pix), f32),
            pltpu.VMEM((own, pix), f32),
        ],
        compiler_params=pltpu.CompilerParams(vmem_limit_bytes=56 * 2**20),
        name="attend",
    )(feat_pad, cot, gain, w_t, wo)


def back_kernel(factor, feat, cot, dq, dkv, att, gain, w_t, w_all, grad_out, sums_out):
    cols, chans = feat.shape[1], feat.shape[2]
    step = pl.program_id(0)

    @pl.when(step == 0)
    def _():
        sums_out[...] = jnp.zeros_like(sums_out)

    x = lanes(feat, 0, range(cols)).astype(f32)
    normed, scaled, inv = normalized(x, gain[...])
    raw = matmul(w_t[...], normed)

    def unit_back(part, grad):
        part_inv = unit_inv(part)
        unit = part * part_inv
        return part_inv * (grad - unit * jnp.mean(grad * unit, axis=0, keepdims=True))

    d_kv = lanes(dkv, 0, range(cols)).astype(f32)
    d_query = unit_back(raw[:chans], lanes(dq, 0, range(cols)).astype(f32))
    d_key = unit_back(raw[chans : 2 * chans], d_kv[:chans])
    raw_grad = jnp.concatenate([d_query, d_key, d_kv[chans:]], axis=0).astype(bf16)
    normed_grad = matmul(w_all[...], raw_grad)
    m = normed_grad * gain[...]
    cot_block = lanes(cot, 0, range(cols))
    branch = inv * (m - scaled * jnp.mean(m * scaled, axis=0, keepdims=True))
    out = (cot_block.astype(f32) + branch).astype(bf16)
    pix = feat.shape[3]
    for c in range(cols):
        grad_out[0, c] = out[:, c * pix : (c + 1) * pix]
    weight = jnp.concatenate(
        [matmul_nt(normed, raw_grad), matmul_nt(lanes(att, 0, range(cols)), cot_block)], axis=1
    )
    sums_out[:chans, :] += weight * factor
    ones = jnp.ones((8, cols * pix), bf16)
    sums_out[chans:, :chans] += matmul_nt(ones, (normed_grad * scaled).astype(bf16)) * factor


def back(factor, feat, cot, dq, dkv, att, gain, w_t, w_all):
    rows, cols, chans, pix = feat.shape

    def by_row(width):
        return pl.BlockSpec((1, cols, width, pix), lambda r: (r, 0, 0, 0))

    def fixed(array):
        return pl.BlockSpec(array.shape, lambda r: (0, 0))

    sums = jax.ShapeDtypeStruct((chans + 8, 4 * chans), f32)
    return pl.pallas_call(
        functools.partial(back_kernel, factor),
        grid=(rows,),
        out_shape=(jax.ShapeDtypeStruct(feat.shape, bf16), sums),
        in_specs=[by_row(chans), by_row(chans), by_row(chans), by_row(2 * chans), by_row(chans)]
        + [fixed(gain), fixed(w_t), fixed(w_all)],
        out_specs=(by_row(chans), fixed(sums)),
        compiler_params=pltpu.CompilerParams(vmem_limit_bytes=32 * 2**20),
        name="back",
    )(feat, cot, dq, dkv, att, gain, w_t, w_all)


def summed(block, axes):
    for axis in axes:
        count = lax.axis_size(axis)
        if count & (count - 1):
            block = lax.psum(block, axis)
            continue
        hop = 1
        while hop < count:
            block = block + lax.ppermute(block, axis, [(i, i ^ hop) for i in range(count)])
            hop *= 2
    return block


def extended(block, axis, dim):
    length = block.shape[dim]
    leading = lax.slice_in_dim(block, 0, REACH, axis=dim)
    last = lax.slice_in_dim(block, length - REACH, length, axis=dim)
    before, after = exchange(leading, last, axis)
    return jnp.concatenate([before, block, after], axis=dim)


def folded(block, axis, dim):
    length = block.shape[dim]
    to_before = lax.slice_in_dim(block, 0, REACH, axis=dim)
    to_after = lax.slice_in_dim(block, length - REACH, length, axis=dim)
    from_before, from_after = exchange(to_before, to_after, axis)
    own = lax.slice_in_dim(block, REACH, length - REACH, axis=dim)
    first = (slice(None),) * dim + (slice(0, REACH),)
    last = (slice(None),) * dim + (slice(own.shape[dim] - REACH, None),)
    return own.at[first].add(from_before).at[last].add(from_after)


def firsts():
    return lax.axis_index("vrow") == 0, lax.axis_index("vcol") == 0


def both_sides(first, block):
    none = jnp.zeros_like(block)
    return jnp.where(first, none, block), jnp.where(first, block, none)


def swap_all(row_block, col_block, corner):
    swap = [(0, 1), (1, 0)]
    return (
        lax.ppermute(col_block, "vcol", swap),
        lax.ppermute(row_block, "vrow", swap),
        lax.ppermute(corner, ("vrow", "vcol"), [(i, 3 - i) for i in range(4)]),
    )


def paired():
    return lax.axis_size("vrow") == 2 and lax.axis_size("vcol") == 2


def extend_views(block):
    if not paired():
        return extended(extended(block, "vrow", 0), "vcol", 1)
    first_r, first_c = firsts()
    row_send = jnp.where(first_r, block[-REACH:], block[:REACH])
    col_send = jnp.where(first_c, block[:, -REACH:], block[:, :REACH])
    corner = jnp.where(first_c, row_send[:, -REACH:], row_send[:, :REACH])
    col, row, corner = swap_all(row_send, col_send, corner)
    left, right = both_sides(first_c, col)
    corner_left, corner_right = both_sides(first_c, corner)
    strip = jnp.concatenate([corner_left, row, corner_right], axis=1)
    above, below = both_sides(first_r, strip)
    middle = jnp.concatenate([left, block, right], axis=1)
    return jnp.concatenate([above, middle, below], axis=0)


def fold_views(block):
    if not paired():
        return folded(folded(block, "vcol", 1), "vrow", 0)
    first_r, first_c = firsts()
    inner = slice(REACH, -REACH)
    strip = jnp.where(first_r, block[-REACH:], block[:REACH])
    col_send = jnp.where(first_c, block[inner, -REACH:], block[inner, :REACH])
    corner = jnp.where(first_c, strip[:, -REACH:], strip[:, :REACH])
    col, row, corner = swap_all(strip[:, inner], col_send, corner)
    corner_left, corner_right = both_sides(first_c, corner)
    row = row.at[:, :REACH].add(corner_left).at[:, -REACH:].add(corner_right)
    left, right = both_sides(first_c, col)
    above, below = both_sides(first_r, row)
    own = block[inner, inner]
    own = own.at[:, :REACH].add(left).at[:, -REACH:].add(right)
    return own.at[:REACH].add(above).at[-REACH:].add(below)


def body(features, out_cotangent, norm_gain, query_proj, keyval_proj, output_proj):
    gain = norm_gain[:, None]
    w_all = jnp.concatenate([query_proj, keyval_proj], axis=1)
    w_t = w_all.T
    feat_pad = extend_views(features)
    dq, att, dkv = attend(feat_pad, out_cotangent, gain, w_t, output_proj)
    dkv = fold_views(dkv)
    rows, cols, chans, pix = features.shape
    axes = ("vrow", "vcol", "pix")
    tokens_all = rows * cols * pix * math.prod(lax.axis_size(a) for a in axes)
    grad, sums = back(
        tokens_all**-0.5, features, out_cotangent, dq, dkv, att, gain, w_t, w_all
    )
    sums = summed(sums, axes[::-1])
    return (
        grad,
        sums[:chans, :chans],
        sums[:chans, chans : 3 * chans],
        sums[:chans, 3 * chans :],
        sums[chans, :chans],
    )


def solution(mesh):
    placed = P("vrow", "vcol", None, "pix")
    return jax.shard_map(
        body,
        mesh=mesh,
        in_specs=(placed, placed, P(), P(), P(), P()),
        out_specs=(placed, P(), P(), P(), P()),
        check_vma=False,
    )
```

```python
import functools
import math

import jax
import jax.numpy as jnp
from jax import lax
from jax.experimental import pallas as pl
from jax.experimental.pallas import tpu as pltpu
from jax.sharding import PartitionSpec as P

HEADS = 4
REACH = 2
SPAN = 2 * REACH + 1
EPSILON = 1e-06
f32, bf16 = jnp.float32, jnp.bfloat16


def shift(block, axis, up):
    count = lax.axis_size(axis)
    pairs = [(i, i + 1) if up else (i + 1, i) for i in range(count - 1)]
    return lax.ppermute(block, axis, pairs)


def exchange(to_before, to_after, axis):
    if lax.axis_size(axis) != 2:
        return shift(to_after, axis, True), shift(to_before, axis, False)
    first = lax.axis_index(axis) == 0
    came = lax.ppermute(jnp.where(first, to_after, to_before), axis, [(0, 1), (1, 0)])
    none = jnp.zeros_like(came)
    return jnp.where(first, none, came), jnp.where(first, came, none)


def lanes(ref, row, cols):
    return jnp.concatenate([ref[row, c] for c in cols], axis=1)


def unit_inv(raw):
    return lax.rsqrt(jnp.mean(raw * raw, axis=0, keepdims=True) + EPSILON)


def matmul(a, b):
    return jnp.dot(a, b, preferred_element_type=f32)


def matmul_nt(a, b):
    return lax.dot_general(a, b, (((1,), (1,)), ((), ())), preferred_element_type=f32)


def normalized(x, gain):
    inv = lax.rsqrt(jnp.mean(x * x, axis=0, keepdims=True) + EPSILON)
    scaled = x * inv
    return (scaled * gain).astype(bf16), scaled, inv


def attend_kernel(
    feat, cot, gain, w_t, wo, dq_out, att_out, dkv_out, q_s, g_s, kv_s, dkv_s, w_s, dp_s, dq_s, att_s
):
    rows, cols, chans, pix = cot.shape
    rows_p, cols_p = feat.shape[:2]
    size = chans // HEADS
    scale = size ** (-0.5)
    kv_row = 2 * chans * cols_p
    q_row = chans * cols
    own = range(REACH, REACH + cols)

    def front(row, _):
        x = lanes(feat, row, range(cols_p)).astype(f32)
        normed, _, _ = normalized(x, gain[...])
        raw = matmul(w_t[...], normed)
        raw_q, raw_k, value = raw[:chans], raw[chans : 2 * chans], raw[2 * chans :]
        query = (raw_q * unit_inv(raw_q)).astype(bf16).astype(f32)
        key = (raw_k * unit_inv(raw_k)).astype(bf16).astype(f32)
        value = value.astype(bf16).astype(f32)
        for c in range(cols_p):
            at = slice(c * pix, (c + 1) * pix)
            kv_s[pl.ds(row * kv_row + c, chans, stride=cols_p), :] = key[:, at]
            kv_s[pl.ds(row * kv_row + chans * cols_p + c, chans, stride=cols_p), :] = value[:, at]
        for i, c in enumerate(own):
            q_s[pl.ds(row * q_row + i, chans, stride=cols), :] = query[:, c * pix : (c + 1) * pix]
        dkv_s[pl.ds(row * kv_row, kv_row), :] = jnp.zeros((kv_row, pix), f32)
        return 0

    lax.fori_loop(0, rows_p, front, 0)

    def grads(row, _):
        out_grad = matmul(wo[...], lanes(cot, row, range(cols)))
        for i in range(cols):
            g_s[pl.ds(row * q_row + i, chans, stride=cols), :] = out_grad[:, i * pix : (i + 1) * pix]
        return 0

    lax.fori_loop(0, rows, grads, 0)

    def one(step, _):
        row, head = step // HEADS, step % HEADS
        q_at = (row + REACH) * q_row + head * size * cols
        g_at = row * q_row + head * size * cols
        q = [q_s[pl.ds(q_at + c * cols, cols), :] for c in range(size)]
        g = [g_s[pl.ds(g_at + c * cols, cols), :] for c in range(size)]
        v_off = chans * cols_p

        def fold(parts):
            while len(parts) > 1:
                parts = [a + b for a, b in zip(parts[::2], parts[1::2])]
            return parts[0]

        def forward(a, carry):
            total, w_dp, att = carry
            base = (row + a) * kv_row + head * size * cols_p
            for b in range(SPAN):
                def k(c):
                    return kv_s[pl.ds(base + (b + c * cols_p), cols), :]

                def v(c):
                    return kv_s[pl.ds(base + (v_off + b + c * cols_p), cols), :]

                w = jnp.exp(fold([q[c] * k(c) for c in range(size)]) * scale)
                dp = fold([g[c] * v(c) for c in range(size)])
                att = [att[c] + w * v(c) for c in range(size)]
                total = total + w
                w_dp = w_dp + w * dp
                at = pl.ds((a * SPAN + b) * cols, cols)
                w_s[at, :] = w
                dp_s[at, :] = dp
            return total, w_dp, att

        zero = jnp.zeros((cols, pix), f32)
        total, w_dp, att = lax.fori_loop(0, SPAN, forward, (zero, zero, [zero] * size))
        inv = 1.0 / total
        spread = w_dp * inv
        for c in range(size):
            att_s[pl.ds(g_at + c * cols, cols), :] = att[c] * inv

        def back(a, dq):
            base = (row + a) * kv_row + head * size * cols_p
            for b in range(SPAN):
                at = pl.ds((a * SPAN + b) * cols, cols)
                p = w_s[at, :] * inv
                ds = p * (dp_s[at, :] - spread) * scale
                dq = [dq[c] + ds * kv_s[pl.ds(base + (b + c * cols_p), cols), :] for c in range(size)]
                for c in range(size):
                    dkv_s[pl.ds(base + (b + c * cols_p), cols), :] += ds * q[c]
                for c in range(size):
                    dkv_s[pl.ds(base + (v_off + b + c * cols_p), cols), :] += p * g[c]
            return dq

        dq = lax.fori_loop(0, SPAN, back, [zero] * size)
        for c in range(size):
            dq_s[pl.ds(g_at + c * cols, cols), :] = dq[c]
        return 0

    lax.fori_loop(0, rows * HEADS, one, 0)

    def finish(row, _):
        for i in range(cols):
            dq_out[row, i] = dq_s[pl.ds(row * q_row + i, chans, stride=cols), :].astype(bf16)
            att_out[row, i] = att_s[pl.ds(row * q_row + i, chans, stride=cols), :].astype(bf16)
        return 0

    lax.fori_loop(0, rows, finish, 0)

    def finish_kv(row, _):
        for c in range(cols_p):
            dkv_out[row, c] = dkv_s[pl.ds(row * kv_row + c, 2 * chans, stride=cols_p), :].astype(bf16)
        return 0

    lax.fori_loop(0, rows_p, finish_kv, 0)


def attend(feat_pad, cot, gain, w_t, wo):
    rows, cols, chans, pix = cot.shape
    rows_p, cols_p = feat_pad.shape[:2]
    own = rows * chans * cols
    pad_kv = rows_p * 2 * chans * cols_p
    whole = pl.BlockSpec(memory_space=pltpu.VMEM)
    return pl.pallas_call(
        attend_kernel,
        out_shape=(
            jax.ShapeDtypeStruct(cot.shape, bf16),
            jax.ShapeDtypeStruct(cot.shape, bf16),
            jax.ShapeDtypeStruct((rows_p, cols_p, 2 * chans, pix), bf16),
        ),
        in_specs=[whole] * 5,
        out_specs=(whole,) * 3,
        scratch_shapes=[
            pltpu.VMEM((rows_p * chans * cols, pix), f32),
            pltpu.VMEM((own, pix), f32),
            pltpu.VMEM((pad_kv, pix), f32),
            pltpu.VMEM((pad_kv, pix), f32),
            pltpu.VMEM((SPAN * SPAN * cols, pix), f32),
            pltpu.VMEM((SPAN * SPAN * cols, pix), f32),
            pltpu.VMEM((own, pix), f32),
            pltpu.VMEM((own, pix), f32),
        ],
        compiler_params=pltpu.CompilerParams(vmem_limit_bytes=56 * 2**20),
        name="attend",
    )(feat_pad, cot, gain, w_t, wo)


def back_kernel(factor, feat, cot, dq, dkv, att, gain, w_t, w_all, grad_out, sums_out):
    cols, chans = feat.shape[1], feat.shape[2]
    step = pl.program_id(0)

    @pl.when(step == 0)
    def _():
        sums_out[...] = jnp.zeros_like(sums_out)

    x = lanes(feat, 0, range(cols)).astype(f32)
    normed, scaled, inv = normalized(x, gain[...])
    raw = matmul(w_t[...], normed)

    def unit_back(part, grad):
        part_inv = unit_inv(part)
        unit = part * part_inv
        return part_inv * (grad - unit * jnp.mean(grad * unit, axis=0, keepdims=True))

    d_kv = lanes(dkv, 0, range(cols)).astype(f32)
    d_query = unit_back(raw[:chans], lanes(dq, 0, range(cols)).astype(f32))
    d_key = unit_back(raw[chans : 2 * chans], d_kv[:chans])
    raw_grad = jnp.concatenate([d_query, d_key, d_kv[chans:]], axis=0).astype(bf16)
    normed_grad = matmul(w_all[...], raw_grad)
    m = normed_grad * gain[...]
    cot_block = lanes(cot, 0, range(cols))
    branch = inv * (m - scaled * jnp.mean(m * scaled, axis=0, keepdims=True))
    out = (cot_block.astype(f32) + branch).astype(bf16)
    pix = feat.shape[3]
    for c in range(cols):
        grad_out[0, c] = out[:, c * pix : (c + 1) * pix]
    weight = jnp.concatenate(
        [matmul_nt(normed, raw_grad), matmul_nt(lanes(att, 0, range(cols)), cot_block)], axis=1
    )
    sums_out[:chans, :] += weight * factor
    ones = jnp.ones((8, cols * pix), bf16)
    sums_out[chans:, :chans] += matmul_nt(ones, (normed_grad * scaled).astype(bf16)) * factor


def back(factor, feat, cot, dq, dkv, att, gain, w_t, w_all):
    rows, cols, chans, pix = feat.shape

    def by_row(width):
        return pl.BlockSpec((1, cols, width, pix), lambda r: (r, 0, 0, 0))

    def fixed(array):
        return pl.BlockSpec(array.shape, lambda r: (0, 0))

    sums = jax.ShapeDtypeStruct((chans + 8, 4 * chans), f32)
    return pl.pallas_call(
        functools.partial(back_kernel, factor),
        grid=(rows,),
        out_shape=(jax.ShapeDtypeStruct(feat.shape, bf16), sums),
        in_specs=[by_row(chans), by_row(chans), by_row(chans), by_row(2 * chans), by_row(chans)]
        + [fixed(gain), fixed(w_t), fixed(w_all)],
        out_specs=(by_row(chans), fixed(sums)),
        compiler_params=pltpu.CompilerParams(vmem_limit_bytes=32 * 2**20),
        name="back",
    )(feat, cot, dq, dkv, att, gain, w_t, w_all)


def summed(block, axes):
    count = math.prod(lax.axis_size(a) for a in axes)
    if count & (count - 1):
        return lax.psum(block, axes)

    def across(hop):
        return lax.ppermute(block, axes, [(i, i ^ hop) for i in range(count)])

    hop = 1
    while hop < count:
        if 4 * hop <= count:
            near, far, corner = across(hop), across(2 * hop), across(3 * hop)
            block = (block + near) + (far + corner)
        else:
            block = block + across(hop)
        hop *= 4
    return block


def extended(block, axis, dim):
    length = block.shape[dim]
    leading = lax.slice_in_dim(block, 0, REACH, axis=dim)
    last = lax.slice_in_dim(block, length - REACH, length, axis=dim)
    before, after = exchange(leading, last, axis)
    return jnp.concatenate([before, block, after], axis=dim)


def folded(block, axis, dim):
    length = block.shape[dim]
    to_before = lax.slice_in_dim(block, 0, REACH, axis=dim)
    to_after = lax.slice_in_dim(block, length - REACH, length, axis=dim)
    from_before, from_after = exchange(to_before, to_after, axis)
    own = lax.slice_in_dim(block, REACH, length - REACH, axis=dim)
    first = (slice(None),) * dim + (slice(0, REACH),)
    last = (slice(None),) * dim + (slice(own.shape[dim] - REACH, None),)
    return own.at[first].add(from_before).at[last].add(from_after)


def firsts():
    return lax.axis_index("vrow") == 0, lax.axis_index("vcol") == 0


def both_sides(first, block):
    none = jnp.zeros_like(block)
    return jnp.where(first, none, block), jnp.where(first, block, none)


def swap_all(row_block, col_block, corner):
    swap = [(0, 1), (1, 0)]
    return (
        lax.ppermute(col_block, "vcol", swap),
        lax.ppermute(row_block, "vrow", swap),
        lax.ppermute(corner, ("vrow", "vcol"), [(i, 3 - i) for i in range(4)]),
    )


def paired():
    return lax.axis_size("vrow") == 2 and lax.axis_size("vcol") == 2


def extend_views(block):
    if not paired():
        return extended(extended(block, "vrow", 0), "vcol", 1)
    first_r, first_c = firsts()
    row_send = jnp.where(first_r, block[-REACH:], block[:REACH])
    col_send = jnp.where(first_c, block[:, -REACH:], block[:, :REACH])
    corner = jnp.where(first_c, row_send[:, -REACH:], row_send[:, :REACH])
    col, row, corner = swap_all(row_send, col_send, corner)
    left, right = both_sides(first_c, col)
    corner_left, corner_right = both_sides(first_c, corner)
    strip = jnp.concatenate([corner_left, row, corner_right], axis=1)
    above, below = both_sides(first_r, strip)
    middle = jnp.concatenate([left, block, right], axis=1)
    return jnp.concatenate([above, middle, below], axis=0)


def fold_views(block):
    if not paired():
        return folded(folded(block, "vcol", 1), "vrow", 0)
    first_r, first_c = firsts()
    inner = slice(REACH, -REACH)
    strip = jnp.where(first_r, block[-REACH:], block[:REACH])
    col_send = jnp.where(first_c, block[inner, -REACH:], block[inner, :REACH])
    corner = jnp.where(first_c, strip[:, -REACH:], strip[:, :REACH])
    col, row, corner = swap_all(strip[:, inner], col_send, corner)
    corner_left, corner_right = both_sides(first_c, corner)
    row = row.at[:, :REACH].add(corner_left).at[:, -REACH:].add(corner_right)
    left, right = both_sides(first_c, col)
    above, below = both_sides(first_r, row)
    own = block[inner, inner]
    own = own.at[:, :REACH].add(left).at[:, -REACH:].add(right)
    return own.at[:REACH].add(above).at[-REACH:].add(below)


def body(features, out_cotangent, norm_gain, query_proj, keyval_proj, output_proj):
    gain = norm_gain[:, None]
    w_all = jnp.concatenate([query_proj, keyval_proj], axis=1)
    w_t = w_all.T
    feat_pad = extend_views(features)
    dq, att, dkv = attend(feat_pad, out_cotangent, gain, w_t, output_proj)
    dkv = fold_views(dkv)
    rows, cols, chans, pix = features.shape
    axes = ("vrow", "vcol", "pix")
    tokens_all = rows * cols * pix * math.prod(lax.axis_size(a) for a in axes)
    grad, sums = back(
        tokens_all**-0.5, features, out_cotangent, dq, dkv, att, gain, w_t, w_all
    )
    sums = summed(sums, axes)
    return (
        grad,
        sums[:chans, :chans],
        sums[:chans, chans : 3 * chans],
        sums[:chans, 3 * chans :],
        sums[chans, :chans],
    )


def solution(mesh):
    placed = P("vrow", "vcol", None, "pix")
    return jax.shard_map(
        body,
        mesh=mesh,
        in_specs=(placed, placed, P(), P(), P(), P()),
        out_specs=(placed, P(), P(), P(), P()),
        check_vma=False,
    )
```
